128 devices in a mesh: row: 8 (over x, z_lo), col: 16 (over y, z_hi, core).
Axes of the slice: x: 4, y: 4, z: 4 (z_hi: 2, z_lo: 2; z = z_hi * 2 + z_lo), core: 2. Of those that a mesh axis runs over, the one named last changes fastest.
Arguments:
- left_factors: bfloat16 [32, 2688, 256], P('row', 'col'), may hold values from -0.59765625 to 0.59765625
- right_factors: bfloat16 [32, 2688, 256], P('row', 'col'), may hold values from -0.5 to 0.5
- ranks: int32 [32], replicated, may hold values from 16 to 256, as said below
Outputs:
- offdiag_update: bfloat16 [32, 32, 2688, 256], P('row', 'col')
- diag_update: bfloat16 [32, 2688, 2688], P('row', 'col')
The draws below stay inside these ranges and needn't reach their ends.
Inputs may be any that keep to these rules, and one draw needn't show every extreme that they name: `ranks`: A tile whose number rnum(p) is 16 or more has rank at most 128, and one such tile has rank exactly 128; some tile of a smaller number has rank 256.
All inputs are finite; a program needn't handle non-finite values.
Results may differ from the reference program's by a relative error of at most 0.0055.
Values may be sent and summed in bfloat16 or wider, within the bound.
No kernel may reach another device: no remote copies, remote signals or barrier semaphores. Data moves between devices by JAX's collectives and lax.ppermute only.
A program may use at most 128 MiB of HBM per device.

```python
import jax
import jax.numpy as jnp
from jax import lax

NB = 2688
R = 256
TR = 4
NT = 32
TC = 2
N_ROW = 8
N_COL = 16


def draw_ranks(key, part):
    key = jax.random.fold_in(key, 7)
    near_key, far_key = jax.random.split(key)
    places = jnp.arange(NT, dtype=jnp.int32)
    number = places % TR * N_ROW + places // TR
    low = max(1, R // 16)
    near_rank = jax.random.randint(near_key, (NT,), low, R + 1, dtype=jnp.int32)
    far_rank = jax.random.randint(far_key, (NT,), low, R // 2 + 1, dtype=jnp.int32)
    split = NT // TC
    result = jnp.where(number < split, near_rank, far_rank)
    result = jnp.where(number == 0, R, result)
    result = jnp.where(number == split, R // 2, result)
    return result.astype(jnp.int32)


def block_scale(key, dims, pieces, smallest, largest):
    def one(dim, parts):
        draws = jax.random.uniform(jax.random.fold_in(jax.random.fold_in(key, 6), dim), (parts,), jnp.float32, smallest / len(pieces), largest / len(pieces))
        return jnp.repeat(jnp.exp(draws), dims[dim] // parts).reshape((-1,) + (1,) * (len(dims) - dim - 1))

    factor_of = one(*pieces[0])
    for cut in pieces[1:]:
        factor_of = factor_of * one(*cut)
    return factor_of


def noise(own_key, dims, width, reach, pieces=(), kind=jnp.bfloat16):
    loudness = block_scale(own_key, dims, pieces, -0.22, 0.18) if pieces else 1.0
    drawn = jax.random.normal(own_key, dims, jnp.float32) * width * loudness
    return jnp.minimum(jnp.maximum(drawn, -reach), reach).astype(kind)


def setup_inputs(seed: int = 0) -> dict:
    key_list = jax.random.split(jax.random.key(seed), 4)
    return {
        "left_factors": noise(key_list[0], (NT, NB, R), 0.1, 0.59765625, ((0, 8), (1, 16))),
        "right_factors": noise(key_list[1], (NT, NB, R), (NB // 16) ** -0.5, 0.5, ((0, 8), (1, 16))),
        "ranks": draw_ranks(jax.random.fold_in(key_list[3], 71), 0),
    }


def reference(left_factors, right_factors, ranks):
    hp = lax.Precision.HIGHEST
    places = jnp.arange(NT, dtype=jnp.int32)
    row_num = (places % TR) * N_ROW + places // TR
    col_num = (places % TC) * N_COL + places // TC
    col_pos = ((col_num % N_ROW) * TR + col_num // N_ROW).astype(jnp.int32)
    keeper = (jnp.arange(R, dtype=jnp.int32)[None, :] < ranks[:, None]).astype(jnp.bfloat16)
    masked = right_factors * keeper[:, None, :]
    col_right = masked[col_pos].astype(jnp.float32)

    def one_row(index):
        vrow = masked[index].astype(jnp.float32)
        urow = left_factors[index].astype(jnp.float32)
        pair = jnp.einsum('nk,qnl->qkl', vrow, col_right, precision=hp).astype(jnp.bfloat16)
        update = jnp.einsum('nk,qkl->qnl', urow, pair.astype(jnp.float32), precision=hp)
        lower = row_num[index] > col_num
        update = jnp.where(lower[:, None, None], update, 0.0).astype(jnp.bfloat16)
        selfpair = jnp.dot(masked[index].T, masked[index], preferred_element_type=jnp.float32).astype(jnp.bfloat16)
        inner = jnp.dot(left_factors[index], selfpair, preferred_element_type=jnp.float32).astype(jnp.bfloat16)
        dense = jnp.dot(inner, left_factors[index].T, preferred_element_type=jnp.float32).astype(jnp.bfloat16)
        return update, dense

    offdiag_update, diag_update = lax.map(one_row, places)
    return offdiag_update, diag_update
```

```python
import functools
import itertools

import jax
import jax.numpy as jnp
from jax import lax
from jax.experimental import pallas as pl
from jax.experimental.pallas import tpu as pltpu
from jax.sharding import PartitionSpec as P

AXES = ("row", "col")
BF, F32 = jnp.bfloat16, jnp.float32
PTS, TILES, LIMIT = 168, 8, 52 * 1024 * 1024


def place(x, zl, y, zh, core):
    return ((x % 4) * 2 + zl) * 16 + (y % 4) * 4 + zh * 2 + core


def mover(rule):
    ranges = (range(4), range(2), range(4), range(2), range(2))
    pairs = [(place(*d), place(*rule(*d))) for d in itertools.product(*ranges)]
    return lambda block: lax.ppermute(block, AXES, pairs)


y_up = mover(lambda x, zl, y, zh, c: (x, zl, y + 1, zh, c))
y_down = mover(lambda x, zl, y, zh, c: (x, zl, y - 1, zh, c))
y_two = mover(lambda x, zl, y, zh, c: (x, zl, y + 2, zh, c))
y_split = mover(lambda x, zl, y, zh, c: (x, zl, y + 1 - 2 * c, zh, c))
z_half = mover(lambda x, zl, y, zh, c: (x, zl, y, 1 - zh, c))
core_swap = mover(lambda x, zl, y, zh, c: (x, zl, y, zh, 1 - c))
x_up = mover(lambda x, zl, y, zh, c: (x + 1, zl, y, zh, c))
x_down = mover(lambda x, zl, y, zh, c: (x - 1, zl, y, zh, c))
x_two = mover(lambda x, zl, y, zh, c: (x + 2, zl, y, zh, c))


def to_column(flip):
    return mover(
        lambda x, zl, y, zh, c: (x + y + 2 * zh + zl, c, x // 2 + 2 * (zh ^ flip), x % 2, zl)
    )


to_column_0, to_column_1 = to_column(0), to_column(1)


def slabs(tiles):
    far = jnp.concatenate([tiles[2, :, :128], tiles[3, :, :128]], axis=1)
    return jnp.stack([tiles[0], tiles[1], far])


def gather(own, core):
    below, above, across = y_up(own), y_down(own), z_half(own)
    first = core == 0
    far = y_split(jnp.where(first, below, above))
    e = y_split(across)
    f = z_half(jnp.where(first, above, below))
    g = y_two(across)
    return [own, below, above, across, far, e, f, g]


def piece_slots(y, zh, core):
    turn = 1 - 2 * core
    moves = ((0, 0), (-1, 0), (1, 0), (0, 1), (2, 0), (-turn, 1), (turn, 1), (2, 1))
    return [(((y + dy) % 4) * 2 + (zh ^ dz)) * 2 + core for dy, dz in moves]


def dot(a, b, ca, cb):
    return lax.dot_general(a, b, (((ca,), (cb,)), ((), ())), preferred_element_type=F32)


def load_pieces(slot_ref, pieces, buf, sem):
    copies = [
        pltpu.make_async_copy(piece, buf.at[slot_ref[i]], sem.at[i]) for i, piece in enumerate(pieces)
    ]
    for copy in copies:
        copy.start()
    return copies


def self_kernel(slot_ref, *refs):
    pieces, out, buf, sem = refs[:16], refs[16], refs[17], refs[18]
    for copy in load_pieces(slot_ref, pieces, buf, sem):
        copy.wait()
    for s in range(3):
        def step(i, acc):
            v = buf[i, s]
            return acc + dot(v, v, 0, 0)

        out[s] = lax.fori_loop(0, 16, step, jnp.zeros((256, 256), F32)).astype(BF)


def diag_kernel(slot_ref, *refs):
    pieces, self_ref, left_ref, full, out, buf, sem = refs[:16], *refs[16:]
    for copy in load_pieces(slot_ref, pieces, buf, sem):
        copy.wait()
    for s in range(3):
        def step(j, _):
            both = [buf[2 * j + k, s].astype(F32) for k in range(2)]
            rows = pl.ds(pl.multiple_of(j * 336, 16), 336)
            full[s, rows, :] = jnp.concatenate(both, axis=0).astype(BF)
            return 0

        lax.fori_loop(0, 8, step, 0)
    for p in range(4):
        if p < 2:
            inner = dot(left_ref[p], self_ref[p], 1, 0).astype(BF)
            out[p] = dot(inner, full[p], 1, 1).astype(BF)
        else:
            cut = slice((p - 2) * 128, (p - 1) * 128)
            inner = dot(left_ref[2, :, cut], self_ref[2, cut, cut], 1, 0).astype(BF)
            out[p] = dot(inner, full[2, :, cut], 1, 1).astype(BF)


STEP = 336


def pair_kernel(slot_ref, col_ref, keep_ref, *refs):
    pieces, cols = refs[:16], refs[16:20]
    full_ref, out, buf, col_buf, pair0, pair1, zero, stage, sem, csem, zsem, osem = refs[20:]
    copies = load_pieces(slot_ref, pieces, buf, sem)
    col_copies = [
        pltpu.make_async_copy(c, col_buf.at[i], csem.at[i]) for i, c in enumerate(cols)
    ]
    for copy in col_copies:
        copy.start()
    zero[...] = jnp.zeros_like(zero)
    zeros = [pltpu.make_async_copy(zero, out.at[p, 1], zsem.at[p]) for p in range(2)]
    for copy in zeros:
        copy.start()
    for copy in copies + col_copies:
        copy.wait()

    pair0[...] = jnp.zeros_like(pair0)
    pair1[...] = jnp.zeros_like(pair1)

    def add(i, _):
        col = col_buf[i // 4, i % 4]
        at = col_ref[i]
        for s in range(3):
            pair0[s] += dot(buf[at, s], col[:, :256], 0, 0)
        pair1[...] += dot(buf[at, 2], col[:, 256:], 0, 0)
        return 0

    lax.fori_loop(0, 16, add, 0)
    ready = []
    for p in range(4):
        rows = slice(0, 256) if p < 2 else slice((p - 2) * 128, (p - 1) * 128)
        both = []
        if p >= 2:
            both.append(jnp.where(keep_ref[2 * p + 1] > 0, pair1[rows], 0.0).astype(BF))
        both.insert(0, jnp.where(keep_ref[2 * p] > 0, pair0[min(p, 2), rows], 0.0).astype(BF))
        ready.append(both)

    def send(i, slot):
        rows = pl.ds(pl.multiple_of(i * STEP, 16), STEP)
        moves = []
        for n, (p, q) in enumerate(((0, 0), (1, 0), (2, 0), (3, 0), (2, 1), (3, 1))):
            moves.append(
                pltpu.make_async_copy(stage.at[slot, n], out.at[p, q, rows], osem.at[slot, n])
            )
        return moves

    steps = 2688 // STEP
    for i in range(steps):
        slot = i % 2
        if i >= 2:
            for copy in send(i - 2, slot):
                copy.wait()
        rows = slice(i * STEP, (i + 1) * STEP)
        for p in range(2):
            stage[slot, p] = dot(full_ref[p, rows], ready[p][0], 1, 0).astype(BF)
        for p in range(2, 4):
            left = full_ref[2, rows, (p - 2) * 128 : (p - 1) * 128]
            stage[slot, p] = dot(left, ready[p][0], 1, 0).astype(BF)
            stage[slot, p + 2, :, :128] = dot(left, ready[p][1], 1, 0).astype(BF)
            if i < 2:
                stage[slot, p + 2, :, 128:] = jnp.zeros((STEP, 128), BF)
        for copy in send(i, slot):
            copy.start()
    for i in range(steps - 2, steps):
        for copy in send(i, i % 2):
            copy.wait()
    for copy in zeros:
        copy.wait()


SMEM = pl.BlockSpec(memory_space=pltpu.SMEM)
VMEM = pl.BlockSpec(memory_space=pltpu.VMEM)
ANY = pl.BlockSpec(memory_space=pl.ANY)


def call(kernel, outs, in_specs, out_specs, scratch, flops, nbytes, args):
    return pl.pallas_call(
        kernel,
        out_shape=outs,
        in_specs=in_specs,
        out_specs=out_specs,
        scratch_shapes=scratch,
        compiler_params=pltpu.CompilerParams(vmem_limit_bytes=LIMIT),
        cost_estimate=pl.CostEstimate(flops=flops, bytes_accessed=nbytes, transcendentals=0),
    )(*args)


def per_device(left_factors, right_factors, ranks):
    row, col = lax.axis_index("row"), lax.axis_index("col")
    x, zl = row // 2, row % 2
    y, zh, core = col // 4, (col // 2) % 2, col % 2
    my_ranks = lax.dynamic_slice_in_dim(ranks, row * 4, 4, 0)
    keeper = (jnp.arange(256, dtype=jnp.int32)[None, :] < my_ranks[:, None]).astype(BF)
    v = slabs(right_factors * keeper[:, None, :])
    u = slabs(left_factors)

    v_other = core_swap(v)
    first = core == 0
    low, high = jnp.where(first, v, v_other), jnp.where(first, v_other, v)

    def column_block(a):
        def one(block):
            near = jnp.where(a == 0, block[0], block[1])
            far = jnp.where(a == 0, block[2, :, :128], block[2, :, 128:])
            return jnp.concatenate([near, far], axis=1)

        return jnp.stack([one(low), one(high)])

    got = jnp.concatenate([to_column_0(column_block(zh)), to_column_1(column_block(1 - zh))])
    cols = [got, x_up(got), x_down(got), x_two(got)]

    v_own = gather(v, core)
    u_own = gather(u, core)
    v_all = v_own + [v_other] + [core_swap(t) for t in v_own[1:]]
    u_all = u_own + [core_swap(t) for t in u_own]
    slots = jnp.stack(piece_slots(y, zh, core) + piece_slots(y, zh, 1 - core)).astype(jnp.int32)

    source = (y % 2) * 2 + zh
    col_slots = []
    for dx in (0, -1, 1, 2):
        for flip in range(2):
            zh_from = (y // 2) ^ flip
            y_from = (x + dx - source - 2 * zh_from - core) % 4
            col_slots += [(y_from * 2 + zh_from) * 2 + k for k in range(2)]
    col_slots = jnp.stack(col_slots).astype(jnp.int32)
    keep = jnp.stack([(p * 8 + row > q * 16 + col) for p in range(4) for q in range(2)])
    keep = keep.astype(jnp.int32)

    pieces = [pltpu.VMEM((16, 3, PTS, 256), BF), pltpu.SemaphoreType.DMA((16,))]
    selfpair = call(
        self_kernel, jax.ShapeDtypeStruct((3, 256, 256), BF), [SMEM] + [ANY] * 16, VMEM, pieces,
        1_100_000_000, 4_500_000, [slots] + v_all,
    )
    full, diag_update = call(
        diag_kernel,
        (jax.ShapeDtypeStruct((3, 2688, 256), BF), jax.ShapeDtypeStruct((4, PTS, 2688), BF)),
        [SMEM] + [ANY] * 16 + [VMEM] * 2, (VMEM, VMEM), pieces,
        1_000_000_000, 12_000_000, [slots] + u_all + [selfpair, u],
    )
    offdiag_update = call(
        pair_kernel,
        jax.ShapeDtypeStruct((4, 2, 2688, 256), BF),
        [SMEM] * 3 + [ANY] * 20 + [VMEM], ANY,
        [
            pltpu.VMEM((16, 3, PTS, 256), BF),
            pltpu.VMEM((4, 4, PTS, 384), BF),
            pltpu.VMEM((3, 256, 256), F32),
            pltpu.VMEM((256, 128), F32),
            pltpu.VMEM((2688, 256), BF),
            pltpu.VMEM((2, 6, STEP, 256), BF),
            pltpu.SemaphoreType.DMA((16,)),
            pltpu.SemaphoreType.DMA((4,)),
            pltpu.SemaphoreType.DMA((2,)),
            pltpu.SemaphoreType.DMA((2, 6)),
        ],
        3_000_000_000, 20_000_000, [slots, col_slots, keep] + v_all + cols + [full],
    )
    return offdiag_update, diag_update


def solution(mesh):
    in_specs = (P("row", "col", None), P("row", "col", None), P())
    out_specs = (P("row", "col", None, None), P("row", "col", None))
    return jax.shard_map(
        per_device, mesh=mesh, in_specs=in_specs, out_specs=out_specs, check_vma=False
    )
```

```python
import itertools

import jax
import jax.numpy as jnp
from jax import lax
from jax.experimental import pallas as pl
from jax.experimental.pallas import tpu as pltpu
from jax.sharding import PartitionSpec as P

AXES = ("row", "col")
BF, F32 = jnp.bfloat16, jnp.float32
PTS, CHIP, NB, LIMIT = 168, 336, 2688, 24 * 1024 * 1024


def place(x, zl, y, zh, core):
    return ((x % 4) * 2 + zl) * 16 + (y % 4) * 4 + zh * 2 + core


def mover(rule):
    ranges = (range(4), range(2), range(4), range(2), range(2))
    pairs = [(place(*d), place(*rule(*d))) for d in itertools.product(*ranges)]
    return lambda block: lax.ppermute(block, AXES, pairs)


y_split = mover(lambda x, zl, y, zh, c: (x, zl, y + 1 - 2 * c, zh, c))
z_half = mover(lambda x, zl, y, zh, c: (x, zl, y, 1 - zh, c))
core_swap = mover(lambda x, zl, y, zh, c: (x, zl, y, zh, 1 - c))
x_up = mover(lambda x, zl, y, zh, c: (x + 1, zl, y, zh, c))
x_down = mover(lambda x, zl, y, zh, c: (x - 1, zl, y, zh, c))
x_split = mover(lambda x, zl, y, zh, c: (x + 1 - 2 * c, zl, y, zh, c))


last_hop = mover(lambda x, zl, y, zh, c: (x, zl, y, 1 - zh, c) if c else (x, zl, y + 2, zh, c))


def to_column(flip):
    def rule(x, zl, y, zh, c):
        return x + y + 2 * c + flip, c, x // 2 + 2 * (zh ^ flip), x % 2, zl

    return mover(rule)


to_column_0, to_column_1 = to_column(0), to_column(1)


def pack_kernel(right_ref, left_ref, out, sem):
    copies = []
    for s, tiles in enumerate((right_ref, left_ref)):
        moves = [(tiles.at[n], out.at[3 * s + n]) for n in range(2)]
        for n in range(2):
            cut = pl.ds(128 * n, 128)
            moves.append((tiles.at[2 + n, :, pl.ds(0, 128)], out.at[3 * s + 2, :, cut]))
        copies += [pltpu.make_async_copy(*move, sem.at[4 * s + n]) for n, move in enumerate(moves)]
    for copy in copies:
        copy.start()
    for copy in copies:
        copy.wait()


def after(block, *others):
    return lax.optimization_barrier((block,) + others)[0]


def dot(a, b, ca, cb):
    return lax.dot_general(a, b, (((ca,), (cb,)), ((), ())), preferred_element_type=F32)


STEP = 672
BLOCKS = ((0, 0), (1, 0), (2, 0), (3, 0), (2, 1), (3, 1))


def block_rows(j):
    return pl.ds(pl.multiple_of(j * CHIP, 16), CHIP)


def within(values, rows, cols):
    k = lax.broadcasted_iota(jnp.int32, values.shape, 0)
    l = lax.broadcasted_iota(jnp.int32, values.shape, 1)
    return jnp.where((k < rows) & (l < cols), values, 0.0).astype(BF)


def where_am_i():
    row, col = lax.axis_index("row"), lax.axis_index("col")
    return row, col, row // 2, row % 2, col // 4, (col // 2) % 2, col % 2


def slot(y, zh, dy, dz):
    return (y + dy + 4) % 4 * 2 + (zh + dz) % 2


def column_slots(dx):
    _, _, x, zl, y, zh, core = where_am_i()
    turned = x + dx - (y % 2) * 2 - zh + 16
    return [(turned - 2 * zl - o) % 4 * 2 + (y // 2 + o) % 2 for o in range(2)]


def partial_kernel(*refs):
    chip, near, near_2, mine, theirs, cols = *refs[:3], refs[3:6], refs[6:8], refs[8:11]
    self_out, pair_out, v_out, col_out, v_buf, col_buf, vsem, csem, osem = refs[11:]
    theirs = (theirs[0], near_2.at[pl.ds(6, 3)], theirs[1])
    _, _, x, zl, y, zh, core = where_am_i()
    turn = 1 - 2 * core

    def piece(src, dy, dz, n):
        rows = block_rows(slot(y, zh, dy, dz))
        return pltpu.make_async_copy(src, v_buf.at[:, rows], vsem.at[n])

    for n, (src, dy) in enumerate(((chip, 0), (near, -turn), (near_2, turn))):
        piece(src.at[pl.ds(0, 3)], dy, 0, n).start()
    for c in range(2):
        @pl.when(core == c)
        def _():
            far_e, across, _ = mine if c == 0 else theirs
            f = theirs[2] if c == 0 else mine[2]
            sources = (across, far_e.at[0], far_e.at[1], f)
            for n, (src, at) in enumerate(zip(sources, ((0, 1), (2, 0), (-1, 1), (1, 1)))):
                piece(src, *at, 3 + n).start()
    copies = []
    for i, dx in enumerate((0, -1, 1)):
        for o, j in enumerate(column_slots(dx)):
            rows = block_rows(j)
            copies.append(
                pltpu.make_async_copy(cols[i].at[o], col_buf.at[rows], csem.at[2 * i + o])
            )
    for copy in copies:
        copy.start()
    for j in column_slots(2):
        col_buf[block_rows(j), :] = jnp.zeros((CHIP, 384), BF)
    last = block_rows(slot(y, zh, 2, 1))
    for s in range(3):
        v_buf[s, last, :] = jnp.zeros((CHIP, 256), BF)
    for n in range(7):
        piece(chip.at[pl.ds(0, 3)], 0, 0, n).wait()
    for copy in copies:
        copy.wait()
    outs = [
        pltpu.make_async_copy(v_buf, v_out, osem.at[0]),
        pltpu.make_async_copy(col_buf, col_out, osem.at[1]),
    ]
    for copy in outs:
        copy.start()
    turned = col_buf[...].T
    for s in range(3):
        size = 256 if s < 2 else 384
        pair_out[:size, s * 256 : (s + 1) * 256] = dot(turned[:size], v_buf[s], 1, 0)
        self_out[s] = dot(v_buf[s], v_buf[s], 0, 0)
    for copy in outs:
        copy.wait()


def final_kernel(rank_ref, *refs):
    chip, near, near_2, left_ref, self_ref, pair_ref, v_in, col_in, last_col = refs[:9]
    mine, theirs = refs[9:13], refs[13:16]
    theirs = (theirs[0], near_2.at[pl.ds(6, 3)], *theirs[1:])
    off, diag = refs[16:18]
    v_buf, u_buf, col_buf, zero, stage, wide, vsem, usem, csem, zsem, osem, dsem = refs[18:]
    row, col, x, zl, y, zh, core = where_am_i()
    turn = 1 - 2 * core

    def piece(src, dy, dz, n):
        rows = block_rows(slot(y, zh, dy, dz))
        return pltpu.make_async_copy(src, u_buf.at[:, rows], usem.at[n])

    at_last = slot(y, zh, 2, 1)
    at_cols = column_slots(2)

    def v_copy(src, n):
        return pltpu.make_async_copy(src, v_buf.at[n], vsem.at[n])

    def col_copy(src, n):
        return pltpu.make_async_copy(src, col_buf.at[n], csem.at[n])

    for n in range(2):
        v_copy(v_in.at[:, block_rows(at_cols[n])], n).start()
        col_copy(last_col.at[n], n).start()

        @pl.when(at_cols[n] == at_last)
        def _():
            col_copy(last_col.at[n], 2).start()

    @pl.when((at_cols[0] != at_last) & (at_cols[1] != at_last))
    def _():
        col_copy(col_in.at[block_rows(at_last)], 2).start()

    for n, (src, dy) in enumerate(((chip, 0), (near, -turn), (near_2, turn))):
        piece(src.at[pl.ds(3, 3)], dy, 0, n).start()
    for c in range(2):
        @pl.when(core == c)
        def _():
            v_copy((mine if c == 0 else theirs)[3], 2).start()
            far_e, across, _, g = theirs if c == 0 else mine
            f = mine[2] if c == 0 else theirs[2]
            sources = (across, far_e.at[0], far_e.at[1], f, g)
            for n, (src, at) in enumerate(zip(sources, ((0, 1), (2, 0), (1, 1), (-1, 1), (2, 1)))):
                piece(src, *at, 3 + n).start()

    zero[...] = jnp.zeros_like(zero)
    zeros = [pltpu.make_async_copy(zero, off.at[p, 1], zsem.at[p]) for p in range(2)]
    for copy in zeros:
        copy.start()
    for i in range(2):
        for n in (4, 5):
            stage[i, n, :, 128:] = jnp.zeros((STEP, 128), BF)
    row_ranks = [rank_ref[row * 4 + p] for p in range(4)]
    col_ranks = [rank_ref[col % 8 * 4 + 2 * q + col // 8] for q in range(2)]

    def kept(p, q):
        return jnp.where(p * 8 + row > q * 16 + col, row_ranks[p], 0)

    for n in range(3):
        v_copy(v_in.at[:, pl.ds(0, CHIP)], n).wait()
        col_copy(last_col.at[0], n).wait()
    turned = [col_buf[n].T for n in range(3)]

    def whole_pair(s, rows):
        total = pair_ref[:rows, s * 256 : (s + 1) * 256] + dot(turned[2][:rows], v_buf[2, s], 1, 0)
        for n in range(2):
            more = dot(turned[n][:rows], v_buf[n, s], 1, 0)
            total += jnp.where(at_cols[n] != at_last, more, 0.0)
        return total.T

    ready = [[within(whole_pair(p, 256), kept(p, 0), col_ranks[0])] for p in range(2)]
    both = whole_pair(2, 384)
    for p in range(2, 4):
        rows = slice((p - 2) * 128, (p - 1) * 128)
        cuts = (slice(0, 256), slice(256, 384))
        ready.append(
            [within(both[rows, cut], kept(p, q), col_ranks[q]) for q, cut in enumerate(cuts)]
        )
    for n in range(8):
        piece(chip.at[pl.ds(3, 3)], 0, 0, n).wait()

    def sends(i):
        rows = slice(i * STEP, (i + 1) * STEP)
        return [
            pltpu.make_async_copy(stage.at[i % 2, n], off.at[p, q, rows], osem.at[i % 2, n])
            for n, (p, q) in enumerate(BLOCKS)
        ]

    steps = NB // STEP
    for i in range(steps):
        if i >= 2:
            for copy in sends(i - 2):
                copy.wait()
        rows = slice(i * STEP, (i + 1) * STEP)
        for p in range(2):
            stage[i % 2, p] = dot(u_buf[p, rows], ready[p][0], 1, 0).astype(BF)
        for p in range(2, 4):
            part = u_buf[2, rows, (p - 2) * 128 : (p - 1) * 128]
            stage[i % 2, p] = dot(part, ready[p][0], 1, 0).astype(BF)
            stage[i % 2, p + 2, :, :128] = dot(part, ready[p][1], 1, 0).astype(BF)
        for copy in sends(i):
            copy.start()

    diag_copies = []
    for p in range(4):
        s = min(p, 2)
        cut = slice(0, 256) if p < 2 else slice((p - 2) * 128, (p - 1) * 128)
        if p < 3:
            own = self_ref[s] + dot(v_buf[2, s], v_buf[2, s], 0, 0)
        square = within(own[cut, cut], row_ranks[p], row_ranks[p])
        inner = dot(left_ref[3 + s, :, cut], square, 1, 0).astype(BF)
        wide[p] = dot(inner, u_buf[s, :, cut], 1, 1).astype(BF)
        diag_copies.append(pltpu.make_async_copy(wide.at[p], diag.at[p], dsem.at[p]))
        diag_copies[-1].start()
    for i in range(steps - 2, steps):
        for copy in sends(i):
            copy.wait()
    for copy in zeros + diag_copies:
        copy.wait()


SMEM = pl.BlockSpec(memory_space=pltpu.SMEM)
VMEM = pl.BlockSpec(memory_space=pltpu.VMEM)
ANY = pl.BlockSpec(memory_space=pl.ANY)


def per_device(left_factors, right_factors, ranks):
    col = lax.axis_index("col")
    zh, core = (col // 2) % 2, col % 2
    first = core == 0
    shape, params = jax.ShapeDtypeStruct, pltpu.CompilerParams(vmem_limit_bytes=LIMIT)
    dma = pltpu.SemaphoreType.DMA
    own = pl.pallas_call(
        pack_kernel,
        out_shape=shape((6, PTS, 256), BF),
        in_specs=[ANY] * 2,
        out_specs=VMEM,
        scratch_shapes=[dma((8,))],
        compiler_params=params,
    )(right_factors, left_factors)
    other = core_swap(own)
    chip = jnp.concatenate([jnp.where(first, own, other), jnp.where(first, other, own)], axis=1)

    def column_block(a):
        near = jnp.where(a == 0, chip[0], chip[1])
        far = jnp.where(a == 0, chip[2, :, :128], chip[2, :, 128:])
        return jnp.concatenate([near, far], axis=1)

    role = jnp.where(first, chip[:3], chip[3:])
    chip, role, block0, block1 = lax.optimization_barrier(
        (chip, role, column_block(zh), column_block(1 - zh))
    )
    near, across = y_split(chip), z_half(role)
    got = jnp.stack([to_column_0(block0), to_column_1(block1)])
    near, across, got = lax.optimization_barrier((near, across, got))
    far_e = y_split(jnp.stack([jnp.where(first, near[:3], near[3:]), across]))
    f = z_half(jnp.where(first, near[3:], near[:3]))
    near_2 = core_swap(jnp.concatenate([near, across]))
    left_col, right_col = x_up(got), x_down(got)
    far_e, f, left_col, right_col = lax.optimization_barrier((far_e, f, left_col, right_col))
    g = last_hop(jnp.where(first, across, far_e[0]))
    last_col = x_split(jnp.where(first, left_col, right_col))
    far_e2, f_2 = core_swap(far_e), core_swap(f)
    selfpart, pairpart, v_full, col_full = pl.pallas_call(
        partial_kernel,
        out_shape=(
            shape((3, 256, 256), F32), shape((384, 768), F32),
            shape((3, NB, 256), BF), shape((NB, 384), BF),
        ),
        in_specs=[ANY] * 11,
        out_specs=(VMEM, VMEM, ANY, ANY),
        scratch_shapes=[
            pltpu.VMEM((3, NB, 256), BF), pltpu.VMEM((NB, 384), BF), dma((7,)), dma((6,)), dma((2,)),
        ],
        compiler_params=params,
        cost_estimate=pl.CostEstimate(
            flops=4_000_000_000, bytes_accessed=15_000_000, transcendentals=0
        ),
    )(chip, near, near_2, far_e, across, f, far_e2, f_2, got, left_col, right_col)
    g_2 = core_swap(after(g, selfpart))
    return pl.pallas_call(
        final_kernel,
        out_shape=(shape((4, 2, NB, 256), BF), shape((4, PTS, NB), BF)),
        in_specs=[SMEM] + [ANY] * 3 + [VMEM] * 3 + [ANY] * 10,
        out_specs=(ANY, ANY),
        scratch_shapes=[
            pltpu.VMEM((3, 3, CHIP, 256), BF),
            pltpu.VMEM((3, NB, 256), BF),
            pltpu.VMEM((3, CHIP, 384), BF),
            pltpu.VMEM((NB, 256), BF),
            pltpu.VMEM((2, 6, STEP, 256), BF),
            pltpu.VMEM((4, PTS, NB), BF),
            dma((3,)), dma((8,)), dma((3,)), dma((2,)), dma((2, 6)), dma((4,)),
        ],
        compiler_params=params,
        cost_estimate=pl.CostEstimate(
            flops=6_000_000_000, bytes_accessed=25_000_000, transcendentals=0
        ),
    )(
        ranks, chip, near, near_2, own, selfpart, pairpart, v_full, col_full, last_col,
        far_e, across, f, g, far_e2, f_2, g_2,
    )


def solution(mesh):
    in_specs = (P("row", "col", None), P("row", "col", None), P())
    out_specs = (P("row", "col", None, None), P("row", "col", None))
    return jax.shard_map(
        per_device, mesh=mesh, in_specs=in_specs, out_specs=out_specs, check_vma=False
    )
```

```python
import itertools

import jax
import jax.numpy as jnp
from jax import lax
from jax.experimental import pallas as pl
from jax.experimental.pallas import tpu as pltpu
from jax.sharding import PartitionSpec as P

AXES = ("row", "col")
BF, F32 = jnp.bfloat16, jnp.float32
PTS, CHIP, NB, LIMIT = 168, 336, 2688, 24 * 1024 * 1024


def place(x, zl, y, zh, core):
    return ((x % 4) * 2 + zl) * 16 + (y % 4) * 4 + zh * 2 + core


def mover(rule):
    ranges = (range(4), range(2), range(4), range(2), range(2))
    pairs = [(place(*d), place(*rule(*d))) for d in itertools.product(*ranges)]
    return lambda block: lax.ppermute(block, AXES, pairs)


y_split = mover(lambda x, zl, y, zh, c: (x, zl, y + 1 - 2 * c, zh, c))
z_half = mover(lambda x, zl, y, zh, c: (x, zl, y, 1 - zh, c))
core_swap = mover(lambda x, zl, y, zh, c: (x, zl, y, zh, 1 - c))
x_up = mover(lambda x, zl, y, zh, c: (x + 1, zl, y, zh, c))
x_down = mover(lambda x, zl, y, zh, c: (x - 1, zl, y, zh, c))
x_split = mover(lambda x, zl, y, zh, c: (x + 1 - 2 * c, zl, y, zh, c))


last_hop = mover(lambda x, zl, y, zh, c: (x, zl, y, 1 - zh, c) if c else (x, zl, y + 2, zh, c))


def to_column(flip):
    def rule(x, zl, y, zh, c):
        return x + y + 2 * c + flip, c, x // 2 + 2 * (zh ^ flip), x % 2, zl

    return mover(rule)


to_column_0, to_column_1 = to_column(0), to_column(1)


def after(block, *others):
    return lax.optimization_barrier((block,) + others)[0]


def dot(a, b, ca, cb):
    return lax.dot_general(a, b, (((ca,), (cb,)), ((), ())), preferred_element_type=F32)


STEP = 672
BLOCKS = ((0, 0), (1, 0), (2, 0), (3, 0), (2, 1), (3, 1))


def block_rows(j):
    return pl.ds(pl.multiple_of(j * CHIP, 16), CHIP)


def within(values, rows, cols):
    k = lax.broadcasted_iota(jnp.int32, values.shape, 0)
    l = lax.broadcasted_iota(jnp.int32, values.shape, 1)
    return jnp.where((k < rows) & (l < cols), values, 0.0).astype(BF)


def where_am_i():
    row, col = lax.axis_index("row"), lax.axis_index("col")
    return row, col, row // 2, row % 2, col // 4, (col // 2) % 2, col % 2


def slot(y, zh, dy, dz):
    return (y + dy + 4) % 4 * 2 + (zh + dz) % 2


def column_slots(dx):
    _, _, x, zl, y, zh, core = where_am_i()
    turned = x + dx - (y % 2) * 2 - zh + 16
    return [(turned - 2 * zl - o) % 4 * 2 + (y // 2 + o) % 2 for o in range(2)]


def partial_kernel(*refs):
    chip, near, near_2, mine, theirs, cols = *refs[:3], refs[3:6], refs[6:8], refs[8:11]
    self_out, pair_out, v_out, col_out, v_buf, col_buf, vsem, csem, osem = refs[11:]
    theirs = (theirs[0], near_2.at[pl.ds(6, 3)], theirs[1])
    _, _, x, zl, y, zh, core = where_am_i()
    turn = 1 - 2 * core

    def piece(src, dy, dz, n):
        rows = block_rows(slot(y, zh, dy, dz))
        return pltpu.make_async_copy(src, v_buf.at[:, rows], vsem.at[n])

    for n, (src, dy) in enumerate(((chip, 0), (near, -turn), (near_2, turn))):
        piece(src.at[pl.ds(0, 3)], dy, 0, n).start()
    for c in range(2):
        @pl.when(core == c)
        def _():
            far_e, across, _ = mine if c == 0 else theirs
            f = theirs[2] if c == 0 else mine[2]
            sources = (across, far_e.at[0], far_e.at[1], f)
            for n, (src, at) in enumerate(zip(sources, ((0, 1), (2, 0), (-1, 1), (1, 1)))):
                piece(src, *at, 3 + n).start()
    copies = []
    for i, dx in enumerate((0, -1, 1)):
        for o, j in enumerate(column_slots(dx)):
            rows = block_rows(j)
            copies.append(
                pltpu.make_async_copy(cols[i].at[o], col_buf.at[rows], csem.at[2 * i + o])
            )
    for copy in copies:
        copy.start()
    for j in column_slots(2):
        col_buf[block_rows(j), :] = jnp.zeros((CHIP, 384), BF)
    last = block_rows(slot(y, zh, 2, 1))
    for s in range(3):
        v_buf[s, last, :] = jnp.zeros((CHIP, 256), BF)
    for n in range(7):
        piece(chip.at[pl.ds(0, 3)], 0, 0, n).wait()
    for copy in copies:
        copy.wait()
    outs = [
        pltpu.make_async_copy(v_buf, v_out, osem.at[0]),
        pltpu.make_async_copy(col_buf, col_out, osem.at[1]),
    ]
    for copy in outs:
        copy.start()
    turned = col_buf[...].T
    for s in range(3):
        size = 256 if s < 2 else 384
        pair_out[:size, s * 256 : (s + 1) * 256] = dot(turned[:size], v_buf[s], 1, 0)
        self_out[s] = dot(v_buf[s], v_buf[s], 0, 0)
    for copy in outs:
        copy.wait()


def final_kernel(rank_ref, *refs):
    chip, near, near_2, left_ref, self_ref, pair_ref, v_in, col_in, last_col = refs[:9]
    mine, theirs = refs[9:13], refs[13:16]
    theirs = (theirs[0], near_2.at[pl.ds(6, 3)], *theirs[1:])
    off, diag = refs[16:18]
    v_buf, u_buf, col_buf, zero, stage, wide, vsem, usem, csem, zsem, osem, dsem = refs[18:]
    row, col, x, zl, y, zh, core = where_am_i()
    turn = 1 - 2 * core

    def piece(src, dy, dz, n):
        rows = block_rows(slot(y, zh, dy, dz))
        return pltpu.make_async_copy(src, u_buf.at[:, rows], usem.at[n])

    at_last = slot(y, zh, 2, 1)
    at_cols = column_slots(2)

    def third(n):
        return pl.ds(n * CHIP, CHIP)

    def v_copy(src, n):
        return pltpu.make_async_copy(src, v_buf.at[:, third(n)], vsem.at[n])

    def col_copy(src, n):
        return pltpu.make_async_copy(src, col_buf.at[third(n)], csem.at[n])

    for n in range(2):
        v_copy(v_in.at[:, block_rows(at_cols[n])], n).start()
        col_copy(last_col.at[n], n).start()

        @pl.when(at_cols[n] == at_last)
        def _():
            col_copy(last_col.at[n], 2).start()

    @pl.when((at_cols[0] != at_last) & (at_cols[1] != at_last))
    def _():
        col_copy(col_in.at[block_rows(at_last)], 2).start()

    for n, (src, dy) in enumerate(((chip, 0), (near, -turn), (near_2, turn))):
        piece(src.at[pl.ds(3, 3)], dy, 0, n).start()
    for c in range(2):
        @pl.when(core == c)
        def _():
            v_copy((mine if c == 0 else theirs)[3], 2).start()
            far_e, across, _, g = theirs if c == 0 else mine
            f = mine[2] if c == 0 else theirs[2]
            sources = (across, far_e.at[0], far_e.at[1], f, g)
            for n, (src, at) in enumerate(zip(sources, ((0, 1), (2, 0), (1, 1), (-1, 1), (2, 1)))):
                piece(src, *at, 3 + n).start()

    zero[...] = jnp.zeros_like(zero)
    zeros = [pltpu.make_async_copy(zero, off.at[p, 1], zsem.at[p]) for p in range(2)]
    for copy in zeros:
        copy.start()
    for n in (4, 5):
        stage[n, :, 128:] = jnp.zeros((NB, 128), BF)
    row_ranks = [rank_ref[row * 4 + p] for p in range(4)]
    col_ranks = [rank_ref[col % 8 * 4 + 2 * q + col // 8] for q in range(2)]

    def kept(p, q):
        return jnp.where(p * 8 + row > q * 16 + col, row_ranks[p], 0)

    for n in range(3):
        v_copy(v_in.at[:, pl.ds(0, CHIP)], n).wait()
        col_copy(last_col.at[0], n).wait()
    for n in range(2):
        @pl.when(at_cols[n] == at_last)
        def _():
            col_buf[third(n), :] = jnp.zeros((CHIP, 384), BF)

    turned = col_buf[...].T

    def whole_pair(s, rows):
        total = pair_ref[:rows, s * 256 : (s + 1) * 256] + dot(turned[:rows], v_buf[s], 1, 0)
        return total.T

    ready = [[within(whole_pair(p, 256), kept(p, 0), col_ranks[0])] for p in range(2)]
    both = whole_pair(2, 384)
    for p in range(2, 4):
        rows = slice((p - 2) * 128, (p - 1) * 128)
        cuts = (slice(0, 256), slice(256, 384))
        ready.append(
            [within(both[rows, cut], kept(p, q), col_ranks[q]) for q, cut in enumerate(cuts)]
        )
    inners = []
    for p in range(4):
        s = min(p, 2)
        cut = slice(0, 256) if p < 2 else slice((p - 2) * 128, (p - 1) * 128)
        if p < 3:
            own = self_ref[s] + dot(v_buf[s, 672:], v_buf[s, 672:], 0, 0)
        square = within(own[cut, cut], row_ranks[p], row_ranks[p])
        inners.append(dot(left_ref[p, :, : cut.stop - cut.start], square, 1, 0).astype(BF))
    for n in range(8):
        piece(chip.at[pl.ds(3, 3)], 0, 0, n).wait()

    out_copies = []

    def send(n):
        p, q = BLOCKS[n]
        out_copies.append(pltpu.make_async_copy(stage.at[n], off.at[p, q], osem.at[n]))
        out_copies[-1].start()

    for p in range(2):
        stage[p] = dot(u_buf[p], ready[p][0], 1, 0).astype(BF)
        send(p)
    for p in range(2, 4):
        both = jnp.concatenate(ready[p], axis=1)
        part = u_buf[2, :, (p - 2) * 128 : (p - 1) * 128]
        both = dot(part, both, 1, 0).astype(BF)
        stage[p] = both[:, :256]
        send(p)
        stage[p + 2, :, :128] = both[:, 256:]
        send(p + 2)

    diag_copies = []
    for p in range(4):
        s = min(p, 2)
        cut = slice(0, 256) if p < 2 else slice((p - 2) * 128, (p - 1) * 128)
        wide[p] = dot(inners[p], u_buf[s, :, cut], 1, 1).astype(BF)
        diag_copies.append(pltpu.make_async_copy(wide.at[p], diag.at[p], dsem.at[p]))
        diag_copies[-1].start()
    for copy in zeros + out_copies + diag_copies:
        copy.wait()


SMEM = pl.BlockSpec(memory_space=pltpu.SMEM)
VMEM = pl.BlockSpec(memory_space=pltpu.VMEM)
ANY = pl.BlockSpec(memory_space=pl.ANY)


def per_device(left_factors, right_factors, ranks):
    col = lax.axis_index("col")
    zh, core = (col // 2) % 2, col % 2
    first = core == 0
    shape, params = jax.ShapeDtypeStruct, pltpu.CompilerParams(vmem_limit_bytes=LIMIT)
    dma = pltpu.SemaphoreType.DMA
    def packed(tiles):
        return jnp.stack(
            [tiles[0], tiles[1], jnp.concatenate([tiles[2, :, :128], tiles[3, :, :128]], axis=1)]
        )

    def chip_block(own, other):
        low, high = jnp.where(first, own, other), jnp.where(first, other, own)
        return jnp.concatenate([packed(low), packed(high)], axis=1)

    other_v, other_u = core_swap(right_factors), core_swap(left_factors)
    chip = jnp.concatenate(
        [chip_block(right_factors, other_v), chip_block(left_factors, other_u)]
    )

    def column_block(a):
        near = jnp.where(a == 0, chip[0], chip[1])
        far = jnp.where(a == 0, chip[2, :, :128], chip[2, :, 128:])
        return jnp.concatenate([near, far], axis=1)

    role = jnp.where(first, chip[:3], chip[3:])
    chip, role, block0, block1 = lax.optimization_barrier(
        (chip, role, column_block(zh), column_block(1 - zh))
    )
    near, across = y_split(chip), z_half(role)
    got = jnp.stack([to_column_0(block0), to_column_1(block1)])
    near, across, got = lax.optimization_barrier((near, across, got))
    far_e = y_split(jnp.stack([jnp.where(first, near[:3], near[3:]), across]))
    f = z_half(jnp.where(first, near[3:], near[:3]))
    near_2 = core_swap(jnp.concatenate([near, across]))
    left_col, right_col = x_up(got), x_down(got)
    far_e, f, left_col, right_col = lax.optimization_barrier((far_e, f, left_col, right_col))
    g = last_hop(jnp.where(first, across, far_e[0]))
    last_col = x_split(jnp.where(first, left_col, right_col))
    far_e2, f_2 = core_swap(far_e), core_swap(f)
    selfpart, pairpart, v_full, col_full = pl.pallas_call(
        partial_kernel,
        out_shape=(
            shape((3, 256, 256), F32), shape((384, 768), F32),
            shape((3, NB, 256), BF), shape((NB, 384), BF),
        ),
        in_specs=[ANY] * 11,
        out_specs=(VMEM, VMEM, ANY, ANY),
        scratch_shapes=[
            pltpu.VMEM((3, NB, 256), BF), pltpu.VMEM((NB, 384), BF), dma((7,)), dma((6,)), dma((2,)),
        ],
        compiler_params=params,
        cost_estimate=pl.CostEstimate(
            flops=4_000_000_000, bytes_accessed=15_000_000, transcendentals=0
        ),
    )(chip, near, near_2, far_e, across, f, far_e2, f_2, got, left_col, right_col)
    g_2 = core_swap(after(g, selfpart))
    return pl.pallas_call(
        final_kernel,
        out_shape=(shape((4, 2, NB, 256), BF), shape((4, PTS, NB), BF)),
        in_specs=[SMEM] + [ANY] * 3 + [VMEM] * 3 + [ANY] * 10,
        out_specs=(ANY, ANY),
        scratch_shapes=[
            pltpu.VMEM((3, 3 * CHIP, 256), BF),
            pltpu.VMEM((3, NB, 256), BF),
            pltpu.VMEM((3 * CHIP, 384), BF),
            pltpu.VMEM((NB, 256), BF),
            pltpu.VMEM((6, NB, 256), BF),
            pltpu.VMEM((4, PTS, NB), BF),
            dma((3,)), dma((8,)), dma((3,)), dma((2,)), dma((6,)), dma((4,)),
        ],
        compiler_params=params,
        cost_estimate=pl.CostEstimate(
            flops=6_000_000_000, bytes_accessed=25_000_000, transcendentals=0
        ),
    )(
        ranks, chip, near, near_2, left_factors, selfpart, pairpart, v_full, col_full, last_col,
        far_e, across, f, g, far_e2, f_2, g_2,
    )


def solution(mesh):
    in_specs = (P("row", "col", None), P("row", "col", None), P())
    out_specs = (P("row", "col", None, None), P("row", "col", None))
    return jax.shard_map(
        per_device, mesh=mesh, in_specs=in_specs, out_specs=out_specs, check_vma=False
    )
```

```python
import itertools

import jax
import jax.numpy as jnp
from jax import lax
from jax.experimental import pallas as pl
from jax.experimental.pallas import tpu as pltpu
from jax.sharding import PartitionSpec as P

AXES = ("row", "col")
BF, F32 = jnp.bfloat16, jnp.float32
PTS, CHIP, NB, LIMIT = 168, 336, 2688, 24 * 1024 * 1024


def place(x, zl, y, zh, core):
    return ((x % 4) * 2 + zl) * 16 + (y % 4) * 4 + zh * 2 + core


def mover(rule):
    ranges = (range(4), range(2), range(4), range(2), range(2))
    pairs = [(place(*d), place(*rule(*d))) for d in itertools.product(*ranges)]
    return lambda block: lax.ppermute(block, AXES, pairs)


y_split = mover(lambda x, zl, y, zh, c: (x, zl, y + 1 - 2 * c, zh, c))
z_half = mover(lambda x, zl, y, zh, c: (x, zl, y, 1 - zh, c))
core_swap = mover(lambda x, zl, y, zh, c: (x, zl, y, zh, 1 - c))
x_up = mover(lambda x, zl, y, zh, c: (x + 1, zl, y, zh, c))
x_down = mover(lambda x, zl, y, zh, c: (x - 1, zl, y, zh, c))
x_split = mover(lambda x, zl, y, zh, c: (x + 1 - 2 * c, zl, y, zh, c))


last_hop = mover(lambda x, zl, y, zh, c: (x, zl, y, 1 - zh, c) if c else (x, zl, y + 2, zh, c))


def to_column(flip):
    def rule(x, zl, y, zh, c):
        return x + y + 2 * c + flip, c, x // 2 + 2 * (zh ^ flip), x % 2, zl

    return mover(rule)


to_column_0, to_column_1 = to_column(0), to_column(1)


def after(block, *others):
    return lax.optimization_barrier((block,) + others)[0]


def dot(a, b, ca, cb):
    return lax.dot_general(a, b, (((ca,), (cb,)), ((), ())), preferred_element_type=F32)


STEP = 672
BLOCKS = ((0, 0), (1, 0), (2, 0), (3, 0), (2, 1), (3, 1))


def block_rows(j):
    return pl.ds(pl.multiple_of(j * CHIP, 16), CHIP)


def within(values, rows, cols):
    k = lax.broadcasted_iota(jnp.int32, values.shape, 0)
    l = lax.broadcasted_iota(jnp.int32, values.shape, 1)
    return jnp.where((k < rows) & (l < cols), values, 0.0).astype(BF)


def where_am_i():
    row, col = lax.axis_index("row"), lax.axis_index("col")
    return row, col, row // 2, row % 2, col // 4, (col // 2) % 2, col % 2


def slot(y, zh, dy, dz):
    return (y + dy + 4) % 4 * 2 + (zh + dz) % 2


def column_slots(dx):
    _, _, x, zl, y, zh, core = where_am_i()
    turned = x + dx - (y % 2) * 2 - zh + 16
    return [(turned - 2 * zl - o) % 4 * 2 + (y // 2 + o) % 2 for o in range(2)]


def partial_kernel(*refs):
    chip, near, near_2, mine, theirs, cols = *refs[:3], refs[3:6], refs[6:8], refs[8:11]
    self_out, pair_out, v_out, col_out, v_buf, col_buf, vsem, csem, osem = refs[11:]
    theirs = (theirs[0], near_2.at[pl.ds(6, 3)], theirs[1])
    _, _, x, zl, y, zh, core = where_am_i()
    turn = 1 - 2 * core

    def piece(src, dy, dz, n):
        rows = block_rows(slot(y, zh, dy, dz))
        return pltpu.make_async_copy(src, v_buf.at[:, rows], vsem.at[n])

    for n, (src, dy) in enumerate(((chip, 0), (near, -turn), (near_2, turn))):
        piece(src.at[pl.ds(0, 3)], dy, 0, n).start()
    for c in range(2):
        @pl.when(core == c)
        def _():
            far_e, across, _ = mine if c == 0 else theirs
            f = theirs[2] if c == 0 else mine[2]
            sources = (across, far_e.at[0], far_e.at[1], f)
            for n, (src, at) in enumerate(zip(sources, ((0, 1), (2, 0), (-1, 1), (1, 1)))):
                piece(src, *at, 3 + n).start()
    copies = []
    for i, dx in enumerate((0, -1, 1)):
        for o, j in enumerate(column_slots(dx)):
            rows = block_rows(j)
            copies.append(
                pltpu.make_async_copy(cols[i].at[o], col_buf.at[rows], csem.at[2 * i + o])
            )
    for copy in copies:
        copy.start()
    for j in column_slots(2):
        col_buf[block_rows(j), :] = jnp.zeros((CHIP, 384), BF)
    last = block_rows(slot(y, zh, 2, 1))
    for s in range(3):
        v_buf[s, last, :] = jnp.zeros((CHIP, 256), BF)
    for n in range(7):
        piece(chip.at[pl.ds(0, 3)], 0, 0, n).wait()
    for copy in copies:
        copy.wait()
    outs = [
        pltpu.make_async_copy(v_buf, v_out, osem.at[0]),
        pltpu.make_async_copy(col_buf, col_out, osem.at[1]),
    ]
    for copy in outs:
        copy.start()
    turned = col_buf[...].T
    for s in range(3):
        size = 256 if s < 2 else 384
        pair_out[:size, s * 256 : (s + 1) * 256] = dot(turned[:size], v_buf[s], 1, 0)
        self_out[s] = dot(v_buf[s], v_buf[s], 0, 0)
    for copy in outs:
        copy.wait()


def late_kernel(pair_ref, v_in, last_col, out, v_buf, col_buf, vsem, csem):
    _, _, _, _, y, zh, _ = where_am_i()
    at_cols = column_slots(2)
    copies = []
    for n in range(2):
        part = pl.ds(n * CHIP, CHIP)
        copies.append(
            pltpu.make_async_copy(v_in.at[:, block_rows(at_cols[n])], v_buf.at[:, part], vsem.at[n])
        )
        copies.append(pltpu.make_async_copy(last_col.at[n], col_buf.at[part], csem.at[n]))
    for copy in copies:
        copy.start()
    for copy in copies:
        copy.wait()
    for n in range(2):
        @pl.when(at_cols[n] == slot(y, zh, 2, 1))
        def _():
            col_buf[pl.ds(n * CHIP, CHIP), :] = jnp.zeros((CHIP, 384), BF)

    turned = col_buf[...].T
    for s in range(3):
        size = 256 if s < 2 else 384
        cut = slice(s * 256, (s + 1) * 256)
        out[:size, cut] = pair_ref[:size, cut] + dot(turned[:size], v_buf[s], 1, 0)


def final_kernel(rank_ref, *refs):
    chip, near, near_2, left_ref, self_ref, pair_ref, col_in, last_col = refs[:8]
    mine, theirs = refs[8:12], refs[12:15]
    theirs = (theirs[0], near_2.at[pl.ds(6, 3)], *theirs[1:])
    off, diag = refs[15:17]
    v_buf, u_buf, col_buf, zero, stage, wide, vsem, usem, csem, zsem, osem, dsem = refs[17:]
    row, col, x, zl, y, zh, core = where_am_i()
    turn = 1 - 2 * core

    def piece(src, dy, dz, n):
        rows = block_rows(slot(y, zh, dy, dz))
        return pltpu.make_async_copy(src, u_buf.at[:, rows], usem.at[n])

    at_last = slot(y, zh, 2, 1)
    at_cols = column_slots(2)

    def col_copy(src):
        return pltpu.make_async_copy(src, col_buf, csem)

    for n in range(2):
        @pl.when(at_cols[n] == at_last)
        def _():
            col_copy(last_col.at[n]).start()

    @pl.when((at_cols[0] != at_last) & (at_cols[1] != at_last))
    def _():
        col_copy(col_in.at[block_rows(at_last)]).start()

    for n, (src, dy) in enumerate(((chip, 0), (near, -turn), (near_2, turn))):
        piece(src.at[pl.ds(3, 3)], dy, 0, n).start()
    for c in range(2):
        @pl.when(core == c)
        def _():
            pltpu.make_async_copy((mine if c == 0 else theirs)[3], v_buf, vsem).start()
            far_e, across, _, g = theirs if c == 0 else mine
            f = mine[2] if c == 0 else theirs[2]
            sources = (across, far_e.at[0], far_e.at[1], f, g)
            for n, (src, at) in enumerate(zip(sources, ((0, 1), (2, 0), (1, 1), (-1, 1), (2, 1)))):
                piece(src, *at, 3 + n).start()

    zero[...] = jnp.zeros_like(zero)
    zeros = [pltpu.make_async_copy(zero, off.at[p, 1], zsem.at[p]) for p in range(2)]
    for copy in zeros:
        copy.start()
    for n in (4, 5):
        stage[n, :, 128:] = jnp.zeros((NB, 128), BF)
    row_ranks = [rank_ref[row * 4 + p] for p in range(4)]
    col_ranks = [rank_ref[col % 8 * 4 + 2 * q + col // 8] for q in range(2)]

    def kept(p, q):
        return jnp.where(p * 8 + row > q * 16 + col, row_ranks[p], 0)

    pltpu.make_async_copy(mine[3], v_buf, vsem).wait()
    col_copy(last_col.at[0]).wait()
    turned = col_buf[...].T

    def whole_pair(s, rows):
        total = pair_ref[:rows, s * 256 : (s + 1) * 256] + dot(turned[:rows], v_buf[s], 1, 0)
        return total.T

    ready = [[within(whole_pair(p, 256), kept(p, 0), col_ranks[0])] for p in range(2)]
    both = whole_pair(2, 384)
    for p in range(2, 4):
        rows = slice((p - 2) * 128, (p - 1) * 128)
        cuts = (slice(0, 256), slice(256, 384))
        ready.append(
            [within(both[rows, cut], kept(p, q), col_ranks[q]) for q, cut in enumerate(cuts)]
        )
    inners = []
    for p in range(4):
        s = min(p, 2)
        cut = slice(0, 256) if p < 2 else slice((p - 2) * 128, (p - 1) * 128)
        if p < 3:
            own = self_ref[s] + dot(v_buf[s], v_buf[s], 0, 0)
        square = within(own[cut, cut], row_ranks[p], row_ranks[p])
        inners.append(dot(left_ref[p, :, : cut.stop - cut.start], square, 1, 0).astype(BF))
    for n in range(8):
        piece(chip.at[pl.ds(3, 3)], 0, 0, n).wait()

    out_copies = []

    def send(n):
        p, q = BLOCKS[n]
        out_copies.append(pltpu.make_async_copy(stage.at[n], off.at[p, q], osem.at[n]))
        out_copies[-1].start()

    for p in range(2):
        stage[p] = dot(u_buf[p], ready[p][0], 1, 0).astype(BF)
        send(p)
    for p in range(2, 4):
        both = jnp.concatenate(ready[p], axis=1)
        part = u_buf[2, :, (p - 2) * 128 : (p - 1) * 128]
        both = dot(part, both, 1, 0).astype(BF)
        stage[p] = both[:, :256]
        send(p)
        stage[p + 2, :, :128] = both[:, 256:]
        send(p + 2)

    diag_copies = []
    for p in range(4):
        s = min(p, 2)
        cut = slice(0, 256) if p < 2 else slice((p - 2) * 128, (p - 1) * 128)
        wide[p] = dot(inners[p], u_buf[s, :, cut], 1, 1).astype(BF)
        diag_copies.append(pltpu.make_async_copy(wide.at[p], diag.at[p], dsem.at[p]))
        diag_copies[-1].start()
    for copy in zeros + out_copies + diag_copies:
        copy.wait()


SMEM = pl.BlockSpec(memory_space=pltpu.SMEM)
VMEM = pl.BlockSpec(memory_space=pltpu.VMEM)
ANY = pl.BlockSpec(memory_space=pl.ANY)


def per_device(left_factors, right_factors, ranks):
    col = lax.axis_index("col")
    zh, core = (col // 2) % 2, col % 2
    first = core == 0
    shape, params = jax.ShapeDtypeStruct, pltpu.CompilerParams(vmem_limit_bytes=LIMIT)
    dma = pltpu.SemaphoreType.DMA
    def packed(tiles):
        return jnp.stack(
            [tiles[0], tiles[1], jnp.concatenate([tiles[2, :, :128], tiles[3, :, :128]], axis=1)]
        )

    def chip_block(own, other):
        low, high = jnp.where(first, own, other), jnp.where(first, other, own)
        return jnp.concatenate([packed(low), packed(high)], axis=1)

    other_v, other_u = core_swap(right_factors), core_swap(left_factors)
    chip = jnp.concatenate(
        [chip_block(right_factors, other_v), chip_block(left_factors, other_u)]
    )

    def column_block(a):
        near = jnp.where(a == 0, chip[0], chip[1])
        far = jnp.where(a == 0, chip[2, :, :128], chip[2, :, 128:])
        return jnp.concatenate([near, far], axis=1)

    role = jnp.where(first, chip[:3], chip[3:])
    chip, role, block0, block1 = lax.optimization_barrier(
        (chip, role, column_block(zh), column_block(1 - zh))
    )
    near, across = y_split(chip), z_half(role)
    got = jnp.stack([to_column_0(block0), to_column_1(block1)])
    near, across, got = lax.optimization_barrier((near, across, got))
    far_e = y_split(jnp.stack([jnp.where(first, near[:3], near[3:]), across]))
    f = z_half(jnp.where(first, near[3:], near[:3]))
    near_2 = core_swap(jnp.concatenate([near, across]))
    left_col, right_col = x_up(got), x_down(got)
    far_e, f, left_col, right_col = lax.optimization_barrier((far_e, f, left_col, right_col))
    g = last_hop(jnp.where(first, across, far_e[0]))
    last_col = x_split(jnp.where(first, left_col, right_col))
    far_e2, f_2 = core_swap(far_e), core_swap(f)
    selfpart, pairpart, v_full, col_full = pl.pallas_call(
        partial_kernel,
        out_shape=(
            shape((3, 256, 256), F32), shape((384, 768), F32),
            shape((3, NB, 256), BF), shape((NB, 384), BF),
        ),
        in_specs=[ANY] * 11,
        out_specs=(VMEM, VMEM, ANY, ANY),
        scratch_shapes=[
            pltpu.VMEM((3, NB, 256), BF), pltpu.VMEM((NB, 384), BF), dma((7,)), dma((6,)), dma((2,)),
        ],
        compiler_params=params,
        cost_estimate=pl.CostEstimate(
            flops=4_000_000_000, bytes_accessed=15_000_000, transcendentals=0
        ),
    )(chip, near, near_2, far_e, across, f, far_e2, f_2, got, left_col, right_col)
    g_2 = core_swap(after(g, selfpart))
    pairpart = pl.pallas_call(
        late_kernel,
        out_shape=shape((384, 768), F32),
        in_specs=[VMEM, ANY, ANY],
        out_specs=VMEM,
        scratch_shapes=[
            pltpu.VMEM((3, 2 * CHIP, 256), BF), pltpu.VMEM((2 * CHIP, 384), BF), dma((2,)), dma((2,)),
        ],
        compiler_params=params,
        cost_estimate=pl.CostEstimate(
            flops=800_000_000, bytes_accessed=4_000_000, transcendentals=0
        ),
    )(pairpart, v_full, last_col)
    return pl.pallas_call(
        final_kernel,
        out_shape=(shape((4, 2, NB, 256), BF), shape((4, PTS, NB), BF)),
        in_specs=[SMEM] + [ANY] * 3 + [VMEM] * 3 + [ANY] * 9,
        out_specs=(ANY, ANY),
        scratch_shapes=[
            pltpu.VMEM((3, CHIP, 256), BF),
            pltpu.VMEM((3, NB, 256), BF),
            pltpu.VMEM((CHIP, 384), BF),
            pltpu.VMEM((NB, 256), BF),
            pltpu.VMEM((6, NB, 256), BF),
            pltpu.VMEM((4, PTS, NB), BF),
            dma, dma((8,)), dma, dma((2,)), dma((6,)), dma((4,)),
        ],
        compiler_params=params,
        cost_estimate=pl.CostEstimate(
            flops=6_000_000_000, bytes_accessed=25_000_000, transcendentals=0
        ),
    )(
        ranks, chip, near, near_2, left_factors, selfpart, pairpart, col_full, last_col,
        far_e, across, f, g, far_e2, f_2, g_2,
    )


def solution(mesh):
    in_specs = (P("row", "col", None), P("row", "col", None), P())
    out_specs = (P("row", "col", None, None), P("row", "col", None))
    return jax.shard_map(
        per_device, mesh=mesh, in_specs=in_specs, out_specs=out_specs, check_vma=False
    )
```

```python
import itertools

import jax
import jax.numpy as jnp
from jax import lax
from jax.experimental import pallas as pl
from jax.experimental.pallas import tpu as pltpu
from jax.sharding import PartitionSpec as P

AXES = ("row", "col")
BF, F32 = jnp.bfloat16, jnp.float32
PTS, CHIP, NB, LIMIT = 168, 336, 2688, 24 * 1024 * 1024


def place(x, zl, y, zh, core):
    return ((x % 4) * 2 + zl) * 16 + (y % 4) * 4 + zh * 2 + core


def mover(rule):
    ranges = (range(4), range(2), range(4), range(2), range(2))
    pairs = [(place(*d), place(*rule(*d))) for d in itertools.product(*ranges)]
    return lambda block: lax.ppermute(block, AXES, pairs)


y_split = mover(lambda x, zl, y, zh, c: (x, zl, y + 1 - 2 * c, zh, c))
z_half = mover(lambda x, zl, y, zh, c: (x, zl, y, 1 - zh, c))
core_swap = mover(lambda x, zl, y, zh, c: (x, zl, y, zh, 1 - c))
x_up = mover(lambda x, zl, y, zh, c: (x + 1, zl, y, zh, c))
x_down = mover(lambda x, zl, y, zh, c: (x - 1, zl, y, zh, c))
x_split = mover(lambda x, zl, y, zh, c: (x + 1 - 2 * c, zl, y, zh, c))


last_hop = mover(lambda x, zl, y, zh, c: (x, zl, y, 1 - zh, c) if c else (x, zl, y + 2, zh, c))


def to_column(flip):
    def rule(x, zl, y, zh, c):
        return x + y + 2 * c + flip, c, x // 2 + 2 * (zh ^ flip), x % 2, zl

    return mover(rule)


to_column_0, to_column_1 = to_column(0), to_column(1)


def after(block, *others):
    return lax.optimization_barrier((block,) + others)[0]


def dot(a, b, ca, cb):
    return lax.dot_general(a, b, (((ca,), (cb,)), ((), ())), preferred_element_type=F32)


STEP = 672
BLOCKS = ((0, 0), (1, 0), (2, 0), (3, 0), (2, 1), (3, 1))


def block_rows(j):
    return pl.ds(pl.multiple_of(j * CHIP, 16), CHIP)


def within(values, rows, cols):
    k = lax.broadcasted_iota(jnp.int32, values.shape, 0)
    l = lax.broadcasted_iota(jnp.int32, values.shape, 1)
    return jnp.where((k < rows) & (l < cols), values, 0.0).astype(BF)


def where_am_i():
    row, col = lax.axis_index("row"), lax.axis_index("col")
    return row, col, row // 2, row % 2, col // 4, (col // 2) % 2, col % 2


def slot(y, zh, dy, dz):
    return (y + dy + 4) % 4 * 2 + (zh + dz) % 2


def column_slots(dx):
    _, _, x, zl, y, zh, core = where_am_i()
    turned = x + dx - (y % 2) * 2 - zh + 16
    return [(turned - 2 * zl - o) % 4 * 2 + (y // 2 + o) % 2 for o in range(2)]


def partial_kernel(*refs):
    chip, near, near_2, mine, theirs, cols = *refs[:3], refs[3:6], refs[6:8], refs[8:11]
    self_out, pair_out, v_out, col_out, v_buf, col_buf, vsem, csem, osem = refs[11:]
    theirs = (theirs[0], near_2.at[pl.ds(6, 3)], theirs[1])
    _, _, x, zl, y, zh, core = where_am_i()
    turn = 1 - 2 * core

    def piece(src, dy, dz, n):
        rows = block_rows(slot(y, zh, dy, dz))
        return pltpu.make_async_copy(src, v_buf.at[:, rows], vsem.at[n])

    for n, (src, dy) in enumerate(((chip, 0), (near, -turn), (near_2, turn))):
        piece(src.at[pl.ds(0, 3)], dy, 0, n).start()
    for c in range(2):
        @pl.when(core == c)
        def _():
            far_e, across, _ = mine if c == 0 else theirs
            f = theirs[2] if c == 0 else mine[2]
            sources = (across, far_e.at[0], far_e.at[1], f)
            for n, (src, at) in enumerate(zip(sources, ((0, 1), (2, 0), (-1, 1), (1, 1)))):
                piece(src, *at, 3 + n).start()
    copies = []
    for i, dx in enumerate((0, -1, 1)):
        for o, j in enumerate(column_slots(dx)):
            rows = block_rows(j)
            copies.append(
                pltpu.make_async_copy(cols[i].at[o], col_buf.at[rows], csem.at[2 * i + o])
            )
    for copy in copies:
        copy.start()
    for j in column_slots(2):
        col_buf[block_rows(j), :] = jnp.zeros((CHIP, 384), BF)
    last = block_rows(slot(y, zh, 2, 1))
    for s in range(3):
        v_buf[s, last, :] = jnp.zeros((CHIP, 256), BF)
    for n in range(7):
        piece(chip.at[pl.ds(0, 3)], 0, 0, n).wait()
    for copy in copies:
        copy.wait()
    outs = [
        pltpu.make_async_copy(v_buf, v_out, osem.at[0]),
        pltpu.make_async_copy(col_buf, col_out, osem.at[1]),
    ]
    for copy in outs:
        copy.start()
    turned = col_buf[...].T
    for s in range(3):
        size = 256 if s < 2 else 384
        pair_out[:size, s * 256 : (s + 1) * 256] = dot(turned[:size], v_buf[s], 1, 0)
        self_out[s] = dot(v_buf[s], v_buf[s], 0, 0)
    for copy in outs:
        copy.wait()


def late_kernel(pair_ref, v_in, last_col, out, v_buf, col_buf, vsem, csem):
    _, _, _, _, y, zh, _ = where_am_i()
    at_cols = column_slots(2)
    copies = []
    for n in range(2):
        part = pl.ds(n * CHIP, CHIP)
        copies.append(
            pltpu.make_async_copy(v_in.at[:, block_rows(at_cols[n])], v_buf.at[:, part], vsem.at[n])
        )
        copies.append(pltpu.make_async_copy(last_col.at[n], col_buf.at[part], csem.at[n]))
    for copy in copies:
        copy.start()
    for copy in copies:
        copy.wait()
    for n in range(2):
        @pl.when(at_cols[n] == slot(y, zh, 2, 1))
        def _():
            col_buf[pl.ds(n * CHIP, CHIP), :] = jnp.zeros((CHIP, 384), BF)

    turned = col_buf[...].T
    for s in range(3):
        size = 256 if s < 2 else 384
        cut = slice(s * 256, (s + 1) * 256)
        out[:size, cut] = pair_ref[:size, cut] + dot(turned[:size], v_buf[s], 1, 0)


def final_kernel(rank_ref, *refs):
    chip, near, near_2, left_ref, self_ref, pair_ref, col_in, last_col = refs[:8]
    mine, theirs = refs[8:12], refs[12:15]
    theirs = (theirs[0], near_2.at[pl.ds(6, 3)], *theirs[1:])
    off, diag = refs[15:17]
    v_buf, u_buf, col_buf, zero, stage, wide, vsem, usem, csem, zsem, osem, dsem = refs[17:]
    row, col, x, zl, y, zh, core = where_am_i()
    turn = 1 - 2 * core

    def piece(src, dy, dz, n):
        rows = block_rows(slot(y, zh, dy, dz))
        return pltpu.make_async_copy(src, u_buf.at[:, rows], usem.at[n])

    at_last = slot(y, zh, 2, 1)
    at_cols = column_slots(2)

    def col_copy(src):
        return pltpu.make_async_copy(src, col_buf, csem)

    for n in range(2):
        @pl.when(at_cols[n] == at_last)
        def _():
            col_copy(last_col.at[n]).start()

    @pl.when((at_cols[0] != at_last) & (at_cols[1] != at_last))
    def _():
        col_copy(col_in.at[block_rows(at_last)]).start()

    for n, (src, dy) in enumerate(((chip, 0), (near, -turn), (near_2, turn))):
        piece(src.at[pl.ds(3, 3)], dy, 0, n).start()
    for c in range(2):
        @pl.when(core == c)
        def _():
            pltpu.make_async_copy((mine if c == 0 else theirs)[3], v_buf, vsem).start()
            far_e, across, _, g = theirs if c == 0 else mine
            f = mine[2] if c == 0 else theirs[2]
            sources = (across, far_e.at[0], far_e.at[1], f, g)
            for n, (src, at) in enumerate(zip(sources, ((0, 1), (2, 0), (1, 1), (-1, 1), (2, 1)))):
                piece(src, *at, 3 + n).start()

    zero[...] = jnp.zeros_like(zero)
    zeros = [pltpu.make_async_copy(zero, off.at[p, 1], zsem.at[p]) for p in range(2)]
    for copy in zeros:
        copy.start()
    for n in (4, 5):
        stage[n, :, 128:] = jnp.zeros((NB, 128), BF)
    row_ranks = [rank_ref[row * 4 + p] for p in range(4)]
    col_ranks = [rank_ref[col % 8 * 4 + 2 * q + col // 8] for q in range(2)]

    def kept(p, q):
        return jnp.where(p * 8 + row > q * 16 + col, row_ranks[p], 0)

    pltpu.make_async_copy(mine[3], v_buf, vsem).wait()
    col_copy(last_col.at[0]).wait()
    turned = col_buf[...].T

    def whole_pair(s, rows):
        return pair_ref[:rows, s * 256 : (s + 1) * 256] + dot(turned[:rows], v_buf[s], 1, 0)

    ready = [[within(whole_pair(p, 256), col_ranks[0], kept(p, 0))] for p in range(2)]
    both = whole_pair(2, 384)
    for p in range(2, 4):
        rows = slice((p - 2) * 128, (p - 1) * 128)
        cuts = (slice(0, 256), slice(256, 384))
        ready.append(
            [within(both[cut, rows], col_ranks[q], kept(p, q)) for q, cut in enumerate(cuts)]
        )
    inners = []
    for p in range(4):
        s = min(p, 2)
        cut = slice(0, 256) if p < 2 else slice((p - 2) * 128, (p - 1) * 128)
        if p < 3:
            own = self_ref[s] + dot(v_buf[s], v_buf[s], 0, 0)
        square = within(own[cut, cut], row_ranks[p], row_ranks[p])
        inners.append(dot(left_ref[p, :, : cut.stop - cut.start], square, 1, 0).astype(BF))
    for n in range(8):
        piece(chip.at[pl.ds(3, 3)], 0, 0, n).wait()

    out_copies = []

    def send(n):
        p, q = BLOCKS[n]
        out_copies.append(pltpu.make_async_copy(stage.at[n], off.at[p, q], osem.at[n]))
        out_copies[-1].start()

    for p in range(2):
        stage[p] = dot(u_buf[p], ready[p][0], 1, 1).astype(BF)
        send(p)
    for p in range(2, 4):
        both = jnp.concatenate(ready[p], axis=0)
        part = u_buf[2, :, (p - 2) * 128 : (p - 1) * 128]
        both = dot(part, both, 1, 1).astype(BF)
        stage[p] = both[:, :256]
        send(p)
        stage[p + 2, :, :128] = both[:, 256:]
        send(p + 2)

    diag_copies = []
    for p in range(4):
        s = min(p, 2)
        cut = slice(0, 256) if p < 2 else slice((p - 2) * 128, (p - 1) * 128)
        wide[p] = dot(inners[p], u_buf[s, :, cut], 1, 1).astype(BF)
        diag_copies.append(pltpu.make_async_copy(wide.at[p], diag.at[p], dsem.at[p]))
        diag_copies[-1].start()
    for copy in zeros + out_copies + diag_copies:
        copy.wait()


SMEM = pl.BlockSpec(memory_space=pltpu.SMEM)
VMEM = pl.BlockSpec(memory_space=pltpu.VMEM)
ANY = pl.BlockSpec(memory_space=pl.ANY)


def per_device(left_factors, right_factors, ranks):
    col = lax.axis_index("col")
    zh, core = (col // 2) % 2, col % 2
    first = core == 0
    shape, params = jax.ShapeDtypeStruct, pltpu.CompilerParams(vmem_limit_bytes=LIMIT)
    dma = pltpu.SemaphoreType.DMA
    def packed(tiles):
        return jnp.stack(
            [tiles[0], tiles[1], jnp.concatenate([tiles[2, :, :128], tiles[3, :, :128]], axis=1)]
        )

    def chip_block(own, other):
        low, high = jnp.where(first, own, other), jnp.where(first, other, own)
        return jnp.concatenate([packed(low), packed(high)], axis=1)

    other_v, other_u = core_swap(right_factors), core_swap(left_factors)
    chip = jnp.concatenate(
        [chip_block(right_factors, other_v), chip_block(left_factors, other_u)]
    )

    def column_block(a):
        near = jnp.where(a == 0, chip[0], chip[1])
        far = jnp.where(a == 0, chip[2, :, :128], chip[2, :, 128:])
        return jnp.concatenate([near, far], axis=1)

    role = jnp.where(first, chip[:3], chip[3:])
    chip, role, block0, block1 = lax.optimization_barrier(
        (chip, role, column_block(zh), column_block(1 - zh))
    )
    near, across = y_split(chip), z_half(role)
    got = jnp.stack([to_column_0(block0), to_column_1(block1)])
    near, across, got = lax.optimization_barrier((near, across, got))
    far_e = y_split(jnp.stack([jnp.where(first, near[:3], near[3:]), across]))
    f = z_half(jnp.where(first, near[3:], near[:3]))
    near_2 = core_swap(jnp.concatenate([near, across]))
    left_col, right_col = x_up(got), x_down(got)
    far_e, f, left_col, right_col = lax.optimization_barrier((far_e, f, left_col, right_col))
    g = last_hop(jnp.where(first, across, far_e[0]))
    last_col = x_split(jnp.where(first, left_col, right_col))
    far_e2, f_2 = core_swap(far_e), core_swap(f)
    selfpart, pairpart, v_full, col_full = pl.pallas_call(
        partial_kernel,
        out_shape=(
            shape((3, 256, 256), F32), shape((384, 768), F32),
            shape((3, NB, 256), BF), shape((NB, 384), BF),
        ),
        in_specs=[ANY] * 11,
        out_specs=(VMEM, VMEM, ANY, ANY),
        scratch_shapes=[
            pltpu.VMEM((3, NB, 256), BF), pltpu.VMEM((NB, 384), BF), dma((7,)), dma((6,)), dma((2,)),
        ],
        compiler_params=params,
        cost_estimate=pl.CostEstimate(
            flops=4_000_000_000, bytes_accessed=15_000_000, transcendentals=0
        ),
    )(chip, near, near_2, far_e, across, f, far_e2, f_2, got, left_col, right_col)
    g_2 = core_swap(after(g, selfpart))
    pairpart = pl.pallas_call(
        late_kernel,
        out_shape=shape((384, 768), F32),
        in_specs=[VMEM, ANY, ANY],
        out_specs=VMEM,
        scratch_shapes=[
            pltpu.VMEM((3, 2 * CHIP, 256), BF), pltpu.VMEM((2 * CHIP, 384), BF), dma((2,)), dma((2,)),
        ],
        compiler_params=params,
        cost_estimate=pl.CostEstimate(
            flops=800_000_000, bytes_accessed=4_000_000, transcendentals=0
        ),
    )(pairpart, v_full, last_col)
    return pl.pallas_call(
        final_kernel,
        out_shape=(shape((4, 2, NB, 256), BF), shape((4, PTS, NB), BF)),
        in_specs=[SMEM] + [ANY] * 3 + [VMEM] * 3 + [ANY] * 9,
        out_specs=(ANY, ANY),
        scratch_shapes=[
            pltpu.VMEM((3, CHIP, 256), BF),
            pltpu.VMEM((3, NB, 256), BF),
            pltpu.VMEM((CHIP, 384), BF),
            pltpu.VMEM((NB, 256), BF),
            pltpu.VMEM((6, NB, 256), BF),
            pltpu.VMEM((4, PTS, NB), BF),
            dma, dma((8,)), dma, dma((2,)), dma((6,)), dma((4,)),
        ],
        compiler_params=params,
        cost_estimate=pl.CostEstimate(
            flops=6_000_000_000, bytes_accessed=25_000_000, transcendentals=0
        ),
    )(
        ranks, chip, near, near_2, left_factors, selfpart, pairpart, col_full, last_col,
        far_e, across, f, g, far_e2, f_2, g_2,
    )


def solution(mesh):
    in_specs = (P("row", "col", None), P("row", "col", None), P())
    out_specs = (P("row", "col", None, None), P("row", "col", None))
    return jax.shard_map(
        per_device, mesh=mesh, in_specs=in_specs, out_specs=out_specs, check_vma=False
    )
```

```python
import itertools

import jax
import jax.numpy as jnp
from jax import lax
from jax.experimental import pallas as pl
from jax.experimental.pallas import tpu as pltpu
from jax.sharding import PartitionSpec as P

AXES = ("row", "col")
BF, F32 = jnp.bfloat16, jnp.float32
PTS, CHIP, NB, LIMIT = 168, 336, 2688, 24 * 1024 * 1024


def place(x, zl, y, zh, core):
    return ((x % 4) * 2 + zl) * 16 + (y % 4) * 4 + zh * 2 + core


def mover(rule):
    ranges = (range(4), range(2), range(4), range(2), range(2))
    pairs = [(place(*d), place(*rule(*d))) for d in itertools.product(*ranges)]
    return lambda block: lax.ppermute(block, AXES, pairs)


y_split = mover(lambda x, zl, y, zh, c: (x, zl, y + 1 - 2 * c, zh, c))
z_half = mover(lambda x, zl, y, zh, c: (x, zl, y, 1 - zh, c))
core_swap = mover(lambda x, zl, y, zh, c: (x, zl, y, zh, 1 - c))
x_up = mover(lambda x, zl, y, zh, c: (x + 1, zl, y, zh, c))
x_down = mover(lambda x, zl, y, zh, c: (x - 1, zl, y, zh, c))
x_split = mover(lambda x, zl, y, zh, c: (x + 1 - 2 * c, zl, y, zh, c))


last_hop = mover(lambda x, zl, y, zh, c: (x, zl, y, 1 - zh, c) if c else (x, zl, y + 2, zh, c))


def to_column(flip):
    def rule(x, zl, y, zh, c):
        return x + y + 2 * c + flip, c, x // 2 + 2 * (zh ^ flip), x % 2, zl

    return mover(rule)


to_column_0, to_column_1 = to_column(0), to_column(1)


def after(block, *others):
    return lax.optimization_barrier((block,) + others)[0]


def dot(a, b, ca, cb):
    return lax.dot_general(a, b, (((ca,), (cb,)), ((), ())), preferred_element_type=F32)


STEP = 672
BLOCKS = ((0, 0), (1, 0), (2, 0), (3, 0), (2, 1), (3, 1))


def block_rows(j):
    return pl.ds(pl.multiple_of(j * CHIP, 16), CHIP)


def within(values, rows, cols):
    k = lax.broadcasted_iota(jnp.int32, values.shape, 0)
    l = lax.broadcasted_iota(jnp.int32, values.shape, 1)
    return jnp.where((k < rows) & (l < cols), values, 0.0).astype(BF)


def where_am_i():
    row, col = lax.axis_index("row"), lax.axis_index("col")
    return row, col, row // 2, row % 2, col // 4, (col // 2) % 2, col % 2


def slot(y, zh, dy, dz):
    return (y + dy + 4) % 4 * 2 + (zh + dz) % 2


def column_slots(dx):
    _, _, x, zl, y, zh, core = where_am_i()
    turned = x + dx - (y % 2) * 2 - zh + 16
    return [(turned - 2 * zl - o) % 4 * 2 + (y // 2 + o) % 2 for o in range(2)]


def partial_kernel(*refs):
    chip, near, near_2, mine, theirs, cols = *refs[:3], refs[3:6], refs[6:8], refs[8:11]
    self_out, pair_out, v_out, col_out, v_buf, col_buf, vsem, csem, osem = refs[11:]
    theirs = (theirs[0], near_2.at[pl.ds(6, 3)], theirs[1])
    _, _, x, zl, y, zh, core = where_am_i()
    turn = 1 - 2 * core

    def piece(src, dy, dz, n):
        rows = block_rows(slot(y, zh, dy, dz))
        return pltpu.make_async_copy(src, v_buf.at[:, rows], vsem.at[n])

    for n, (src, dy) in enumerate(((chip, 0), (near, -turn), (near_2, turn))):
        piece(src.at[pl.ds(0, 3)], dy, 0, n).start()
    for c in range(2):
        @pl.when(core == c)
        def _():
            far_e, across, _ = mine if c == 0 else theirs
            f = theirs[2] if c == 0 else mine[2]
            sources = (across, far_e.at[0], far_e.at[1], f)
            for n, (src, at) in enumerate(zip(sources, ((0, 1), (2, 0), (-1, 1), (1, 1)))):
                piece(src, *at, 3 + n).start()
    copies = []
    for i, dx in enumerate((0, -1, 1)):
        for o, j in enumerate(column_slots(dx)):
            rows = block_rows(j)
            copies.append(
                pltpu.make_async_copy(cols[i].at[o], col_buf.at[rows], csem.at[2 * i + o])
            )
    for copy in copies:
        copy.start()
    for j in column_slots(2):
        col_buf[block_rows(j), :] = jnp.zeros((CHIP, 384), BF)
    last = block_rows(slot(y, zh, 2, 1))
    for s in range(3):
        v_buf[s, last, :] = jnp.zeros((CHIP, 256), BF)
    for n in range(7):
        piece(chip.at[pl.ds(0, 3)], 0, 0, n).wait()
    for copy in copies:
        copy.wait()
    outs = [
        pltpu.make_async_copy(v_buf, v_out, osem.at[0]),
        pltpu.make_async_copy(col_buf, col_out, osem.at[1]),
    ]
    for copy in outs:
        copy.start()
    turned = col_buf[...].T
    for s in range(3):
        size = 256 if s < 2 else 384
        pair_out[:size, s * 256 : (s + 1) * 256] = dot(turned[:size], v_buf[s], 1, 0)
        self_out[s] = dot(v_buf[s], v_buf[s], 0, 0)
    for copy in outs:
        copy.wait()


def late_kernel(pair_ref, v_in, last_col, out, v_buf, col_buf, vsem, csem):
    _, _, _, _, y, zh, _ = where_am_i()
    at_cols = column_slots(2)
    copies = []
    for n in range(2):
        part = pl.ds(n * CHIP, CHIP)
        copies.append(
            pltpu.make_async_copy(v_in.at[:, block_rows(at_cols[n])], v_buf.at[:, part], vsem.at[n])
        )
        copies.append(pltpu.make_async_copy(last_col.at[n], col_buf.at[part], csem.at[n]))
    for copy in copies:
        copy.start()
    for copy in copies:
        copy.wait()
    for n in range(2):
        @pl.when(at_cols[n] == slot(y, zh, 2, 1))
        def _():
            col_buf[pl.ds(n * CHIP, CHIP), :] = jnp.zeros((CHIP, 384), BF)

    turned = col_buf[...].T
    for s in range(3):
        size = 256 if s < 2 else 384
        cut = slice(s * 256, (s + 1) * 256)
        out[:size, cut] = pair_ref[:size, cut] + dot(turned[:size], v_buf[s], 1, 0)


def final_kernel(rank_ref, *refs):
    chip, near, near_2, left_ref, self_ref, pair_ref, col_in, last_col = refs[:8]
    mine, theirs = refs[8:12], refs[12:15]
    theirs = (theirs[0], near_2.at[pl.ds(6, 3)], *theirs[1:])
    off, diag = refs[15:17]
    v_buf, u_buf, col_buf, zero, stage, wide, vsem, usem, csem, zsem, osem, dsem = refs[17:]
    row, col, x, zl, y, zh, core = where_am_i()
    turn = 1 - 2 * core

    def piece(src, dy, dz, n):
        rows = block_rows(slot(y, zh, dy, dz))
        return pltpu.make_async_copy(src, u_buf.at[:, rows], usem.at[n])

    at_last = slot(y, zh, 2, 1)
    at_cols = column_slots(2)

    def col_copy(src):
        return pltpu.make_async_copy(src, col_buf, csem)

    for n in range(2):
        @pl.when(at_cols[n] == at_last)
        def _():
            col_copy(last_col.at[n]).start()

    @pl.when((at_cols[0] != at_last) & (at_cols[1] != at_last))
    def _():
        col_copy(col_in.at[block_rows(at_last)]).start()

    for n, (src, dy) in enumerate(((chip, 0), (near, -turn), (near_2, turn))):
        piece(src.at[pl.ds(3, 3)], dy, 0, n).start()
    for c in range(2):
        @pl.when(core == c)
        def _():
            pltpu.make_async_copy((mine if c == 0 else theirs)[3], v_buf, vsem).start()
            far_e, across, _, g = theirs if c == 0 else mine
            f = mine[2] if c == 0 else theirs[2]
            sources = (across, far_e.at[0], far_e.at[1], f, g)
            for n, (src, at) in enumerate(zip(sources, ((0, 1), (2, 0), (1, 1), (-1, 1), (2, 1)))):
                piece(src, *at, 3 + n).start()

    zero[...] = jnp.zeros_like(zero)
    zeros = [pltpu.make_async_copy(zero, off.at[p, 1], zsem.at[p]) for p in range(2)]
    for n in (4, 5):
        stage[n, :, 128:] = jnp.zeros((NB, 128), BF)
    row_ranks = [rank_ref[row * 4 + p] for p in range(4)]
    col_ranks = [rank_ref[col % 8 * 4 + 2 * q + col // 8] for q in range(2)]

    def kept(p, q):
        return jnp.where(p * 8 + row > q * 16 + col, row_ranks[p], 0)

    pltpu.make_async_copy(mine[3], v_buf, vsem).wait()
    col_copy(last_col.at[0]).wait()
    turned = col_buf[...].T

    def whole_pair(s, rows):
        return pair_ref[:rows, s * 256 : (s + 1) * 256] + dot(turned[:rows], v_buf[s], 1, 0)

    ready = [[within(whole_pair(p, 256), col_ranks[0], kept(p, 0))] for p in range(2)]
    both = whole_pair(2, 384)
    for p in range(2, 4):
        rows = slice((p - 2) * 128, (p - 1) * 128)
        cuts = (slice(0, 256), slice(256, 384))
        ready.append(
            [within(both[cut, rows], col_ranks[q], kept(p, q)) for q, cut in enumerate(cuts)]
        )
    inners = []
    for p in range(4):
        s = min(p, 2)
        cut = slice(0, 256) if p < 2 else slice((p - 2) * 128, (p - 1) * 128)
        if p < 3:
            own = self_ref[s] + dot(v_buf[s], v_buf[s], 0, 0)
        square = within(own[cut, cut], row_ranks[p], row_ranks[p])
        inners.append(dot(left_ref[p, :, : cut.stop - cut.start], square, 1, 0).astype(BF))
    for n in range(8):
        piece(chip.at[pl.ds(3, 3)], 0, 0, n).wait()
    for copy in zeros:
        copy.start()

    out_copies = []

    def send(n):
        p, q = BLOCKS[n]
        out_copies.append(pltpu.make_async_copy(stage.at[n], off.at[p, q], osem.at[n]))
        out_copies[-1].start()

    for p in range(2):
        stage[p] = dot(u_buf[p], ready[p][0], 1, 1).astype(BF)
        send(p)
    for p in range(2, 4):
        both = jnp.concatenate(ready[p], axis=0)
        part = u_buf[2, :, (p - 2) * 128 : (p - 1) * 128]
        both = dot(part, both, 1, 1).astype(BF)
        stage[p] = both[:, :256]
        send(p)
        stage[p + 2, :, :128] = both[:, 256:]
        send(p + 2)

    diag_copies = []
    for p in range(4):
        s = min(p, 2)
        cut = slice(0, 256) if p < 2 else slice((p - 2) * 128, (p - 1) * 128)
        wide[p] = dot(inners[p], u_buf[s, :, cut], 1, 1).astype(BF)
        diag_copies.append(pltpu.make_async_copy(wide.at[p], diag.at[p], dsem.at[p]))
        diag_copies[-1].start()
    for copy in zeros + out_copies + diag_copies:
        copy.wait()


SMEM = pl.BlockSpec(memory_space=pltpu.SMEM)
VMEM = pl.BlockSpec(memory_space=pltpu.VMEM)
ANY = pl.BlockSpec(memory_space=pl.ANY)


def per_device(left_factors, right_factors, ranks):
    col = lax.axis_index("col")
    zh, core = (col // 2) % 2, col % 2
    first = core == 0
    shape, params = jax.ShapeDtypeStruct, pltpu.CompilerParams(vmem_limit_bytes=LIMIT)
    dma = pltpu.SemaphoreType.DMA
    def packed(tiles):
        return jnp.stack(
            [tiles[0], tiles[1], jnp.concatenate([tiles[2, :, :128], tiles[3, :, :128]], axis=1)]
        )

    def chip_block(own, other):
        low, high = jnp.where(first, own, other), jnp.where(first, other, own)
        return jnp.concatenate([packed(low), packed(high)], axis=1)

    other_v, other_u = core_swap(right_factors), core_swap(left_factors)
    chip = jnp.concatenate(
        [chip_block(right_factors, other_v), chip_block(left_factors, other_u)]
    )

    def column_block(a):
        near = jnp.where(a == 0, chip[0], chip[1])
        far = jnp.where(a == 0, chip[2, :, :128], chip[2, :, 128:])
        return jnp.concatenate([near, far], axis=1)

    role = jnp.where(first, chip[:3], chip[3:])
    chip, role, block0, block1 = lax.optimization_barrier(
        (chip, role, column_block(zh), column_block(1 - zh))
    )
    near, across = y_split(chip), z_half(role)
    got = jnp.stack([to_column_0(block0), to_column_1(block1)])
    near, across, got = lax.optimization_barrier((near, across, got))
    far_e = y_split(jnp.stack([jnp.where(first, near[:3], near[3:]), across]))
    f = z_half(jnp.where(first, near[3:], near[:3]))
    near_2 = core_swap(jnp.concatenate([near, across]))
    left_col, right_col = x_up(got), x_down(got)
    far_e, f, left_col, right_col = lax.optimization_barrier((far_e, f, left_col, right_col))
    g = last_hop(jnp.where(first, across, far_e[0]))
    last_col = x_split(jnp.where(first, left_col, right_col))
    far_e2, f_2 = core_swap(far_e), core_swap(f)
    selfpart, pairpart, v_full, col_full = pl.pallas_call(
        partial_kernel,
        out_shape=(
            shape((3, 256, 256), F32), shape((384, 768), F32),
            shape((3, NB, 256), BF), shape((NB, 384), BF),
        ),
        in_specs=[ANY] * 11,
        out_specs=(VMEM, VMEM, ANY, ANY),
        scratch_shapes=[
            pltpu.VMEM((3, NB, 256), BF), pltpu.VMEM((NB, 384), BF), dma((7,)), dma((6,)), dma((2,)),
        ],
        compiler_params=params,
        cost_estimate=pl.CostEstimate(
            flops=4_000_000_000, bytes_accessed=15_000_000, transcendentals=0
        ),
    )(chip, near, near_2, far_e, across, f, far_e2, f_2, got, left_col, right_col)
    g_2 = core_swap(after(g, selfpart))
    pairpart = pl.pallas_call(
        late_kernel,
        out_shape=shape((384, 768), F32),
        in_specs=[VMEM, ANY, ANY],
        out_specs=VMEM,
        scratch_shapes=[
            pltpu.VMEM((3, 2 * CHIP, 256), BF), pltpu.VMEM((2 * CHIP, 384), BF), dma((2,)), dma((2,)),
        ],
        compiler_params=params,
        cost_estimate=pl.CostEstimate(
            flops=800_000_000, bytes_accessed=4_000_000, transcendentals=0
        ),
    )(pairpart, v_full, last_col)
    return pl.pallas_call(
        final_kernel,
        out_shape=(shape((4, 2, NB, 256), BF), shape((4, PTS, NB), BF)),
        in_specs=[SMEM] + [ANY] * 3 + [VMEM] * 3 + [ANY] * 9,
        out_specs=(ANY, ANY),
        scratch_shapes=[
            pltpu.VMEM((3, CHIP, 256), BF),
            pltpu.VMEM((3, NB, 256), BF),
            pltpu.VMEM((CHIP, 384), BF),
            pltpu.VMEM((NB, 256), BF),
            pltpu.VMEM((6, NB, 256), BF),
            pltpu.VMEM((4, PTS, NB), BF),
            dma, dma((8,)), dma, dma((2,)), dma((6,)), dma((4,)),
        ],
        compiler_params=params,
        cost_estimate=pl.CostEstimate(
            flops=6_000_000_000, bytes_accessed=25_000_000, transcendentals=0
        ),
    )(
        ranks, chip, near, near_2, left_factors, selfpart, pairpart, col_full, last_col,
        far_e, across, f, g, far_e2, f_2, g_2,
    )


def solution(mesh):
    in_specs = (P("row", "col", None), P("row", "col", None), P())
    out_specs = (P("row", "col", None, None), P("row", "col", None))
    return jax.shard_map(
        per_device, mesh=mesh, in_specs=in_specs, out_specs=out_specs, check_vma=False
    )
```
